1024 devices in a mesh: node: 64 (over x, y, core), local: 16 (over z).
Axes of the slice: x: 4, y: 8, z: 16, core: 2. Of those that a mesh axis runs over, the one named last changes fastest.
Arguments:
- tokens: bfloat16 [2048, 3584], P('node', 'local'), may hold values from -6 to 6
- grad_out: bfloat16 [2048, 3584], P('node', 'local'), may hold values from -6 to 6
- route_prob: bfloat16 [2048, 4], P('node'), may hold values from 0.049804688 to 0.59765625
- route_expert: int32 [2048, 4], P('node'), may hold values from 0 to 63, all different within a row; in each aligned block of 32 rows (0 to 31, 32 to 63, ...) at most 4 rows name the same one
- w_gate: bfloat16 [64, 3584, 2048], P('node', 'local'), may hold values from -0.125 to 0.125
- w_up: bfloat16 [64, 3584, 2048], P('node', 'local'), may hold values from -0.125 to 0.125
- w_down: bfloat16 [64, 2048, 3584], P('node', None, 'local'), may hold values from -0.09375 to 0.09375
Outputs:
- grad_tokens: bfloat16 [2048, 3584], P('node', 'local')
- grad_prob: bfloat16 [2048, 4], P('node')
The draws below stay inside these ranges and needn't reach their ends.
Inputs may be any that keep to these rules, and one draw needn't show every extreme that they name: `route_expert`: each row names 4 different experts; in each block of 32 rows no expert is named by more than 4 rows, a bound that some block reaches.
All inputs are finite; a program needn't handle non-finite values.
Results may differ from the reference program's by a relative error of at most 0.022.
Values may be sent and summed in bfloat16 or wider, within the bound.
A program may use at most 32 MiB of HBM per device.

```python
import math
import jax
import jax.numpy as jnp
import numpy as np
from jax import lax

D = 3584
F = 2048
TOPK = 4
CAP = 4
EXPERTS = 64
TOK_NODE = 32
TOKENS = 2048
N_NODE = 64


def with_spikes(drawn, own_key, source, target, shards_of, factor):
    owner, partner = [(jnp.arange(drawn.shape[axis_at]) // (drawn.shape[axis_at] // shards_of)).reshape([-1 if axis == axis_at else 1 for axis in range(drawn.ndim)]) for axis_at in (source, target)]
    chosen = jax.random.permutation(own_key, shards_of)[partner]
    strong = (owner == chosen) | (owner == (partner + shards_of // 2) % shards_of)
    return jnp.where(strong, factor * drawn, drawn)


def steps_of(stream_key, dims, cuts, least, high):
    loudness = 1.0
    for dim, shards_of in cuts:
        steps = jax.random.uniform(jax.random.fold_in(jax.random.fold_in(stream_key, 6), dim), (shards_of,), jnp.float32, least / len(cuts), high / len(cuts))
        loudness = loudness * jnp.repeat(jnp.exp(steps), dims[dim] // shards_of).reshape((-1,) + (1,) * (len(dims) - 1 - dim))
    return loudness


def routed_block(own_key, own, number, rows, count, top, limit, slope):
    ranking = jax.random.permutation(own_key, count)
    crowded, usual = shares(count, rows * top, limit, slope, True), shares(count, rows * top, limit, slope, False)
    places = jnp.arange(count)

    def named(sizes, rotation):
        used = int((sizes > 0).sum())
        fixed = max(1, used // 4)
        shifted = fixed + (places - fixed + rotation * (used - fixed)) % max(1, count - fixed)
        return jnp.zeros((count,), jnp.int32).at[ranking[jnp.where(places < fixed, places, shifted)]].set(jnp.asarray(sizes, jnp.int32))

    sizes = jnp.where(number % 4 == 0, named(crowded, number // 4), named(usual, number - number // 4 - 1))
    mixed = jax.random.permutation(jax.random.fold_in(own, 3), count)
    source_of, sink = mixed[0:count // 2 * 2:2], mixed[1:count // 2 * 2:2]
    margin = jnp.minimum(sizes[source_of] - 1, limit - sizes[sink]) // 2
    margin = jnp.where((source_of == ranking[0]) | (sink == ranking[0]) | (sizes[sink] == 0), 0, jnp.maximum(margin, 0))
    shifted = jax.random.randint(jax.random.fold_in(own, 4), (count // 2,), 0, 1 << 20) % (margin + 1)
    sizes = sizes.at[source_of].add(-shifted).at[sink].add(shifted)
    items = jnp.searchsorted(jnp.cumsum(sizes), jnp.arange(rows * top), side="right").astype(jnp.int32)
    grid = items.reshape(top, rows).T
    grid = grid[jax.random.permutation(jax.random.fold_in(own, 1), rows)]
    rotation = jax.random.randint(jax.random.fold_in(own, 2), (rows, 1), 0, top)
    return jnp.take_along_axis(grid, (jnp.arange(top)[None, :] + rotation) % top, axis=1)


def shares(amount, total, bound, skew, full):
    loads = [(1 << 20) // math.isqrt(grade ** skew) + 1 for grade in range(1, amount + 1)]
    largest = bound if full else min(bound, max(-(-total // amount), total * loads[0] // sum(loads)))
    least = 1 if total - largest >= amount - 1 else 0
    given, rest = [largest] + [least] * (amount - 1), total - largest - least * (amount - 1)
    while rest > 0:
        candidates = [i for i in range(1, amount) if given[i] < largest] or [i for i in range(1, amount) if given[i] < bound]
        whole, remaining = sum([loads[i] for i in candidates]), rest
        for i in candidates:
            extra = min(bound - given[i], max(1, remaining * loads[i] // whole), rest)
            given[i] = given[i] + extra
            rest = rest - extra
    return np.array(given)


def bell_draw(key, shape, deviation, bound, cuts=(), kind=jnp.bfloat16):
    array = jax.random.normal(key, shape, jnp.float32) * deviation
    if len(cuts) > 0:
        array = steps_of(key, shape, cuts, -0.22, 0.18) * array
    return jnp.clip(array, min=-bound, max=bound).astype(kind)


def noise_with(rng, dims, width, reach, split, heavy, held_as=jnp.bfloat16):
    drawn = width * jax.random.normal(rng, dims, jnp.float32)
    if split:
        drawn = drawn * steps_of(rng, dims, split, -0.22, 0.18)
    return jnp.clip(with_spikes(drawn, jax.random.fold_in(rng, 3), *heavy), -reach, reach).astype(held_as)


def setup_inputs(seed: int = 0) -> dict:
    key_of = jax.random.split(jax.random.key(seed), 8)
    tokens = bell_draw(key_of[0], (TOKENS, D), 1.0, 6.0, ((0, 64), (1, 16)))
    grad_out = bell_draw(key_of[1], (TOKENS, D), 1.0, 6.0, ((0, 64), (1, 16)))
    route_prob = jnp.clip(0.049804688 + 0.54785156 * jax.random.uniform(key_of[2], (TOKENS, TOPK), jnp.float32) ** steps_of(key_of[2], (TOKENS, TOPK), ((0, 64),), -0.2, 0.2), 0.049804688, 0.59765625).astype(jnp.bfloat16)
    route_expert_keys = jax.random.split(jax.random.fold_in(key_of[3], 1), TOKENS // TOK_NODE)
    route_expert_turns = jax.random.permutation(jax.random.fold_in(key_of[3], 3), TOKENS // TOK_NODE)
    route_expert = jax.vmap(lambda own, number: routed_block(jax.random.fold_in(key_of[3], 2), own, number, TOK_NODE, EXPERTS, TOPK, CAP, 2))(route_expert_keys, route_expert_turns).reshape((TOKENS, TOPK))
    w_gate = noise_with(key_of[4], (EXPERTS, D, F), D ** -0.5, 0.125, ((0, 64), (1, 16)), (1, 2, 16, 2.0))
    w_up = noise_with(key_of[5], (EXPERTS, D, F), D ** -0.5, 0.125, ((0, 64), (1, 16)), (1, 2, 16, 2.0))
    w_down = noise_with(key_of[6], (EXPERTS, F, D), (4 * F) ** -0.5, 0.09375, ((0, 64), (2, 16)), (2, 1, 16, 2.0))
    return dict(tokens=tokens, grad_out=grad_out, route_prob=route_prob, route_expert=route_expert, w_gate=w_gate, w_up=w_up, w_down=w_down)


def route_slots(block_routes, experts, capacity):
    flat_ids = block_routes.reshape(-1)
    onehot = (flat_ids[:, None] == jnp.arange(experts, dtype=jnp.int32)[None, :]).astype(jnp.int32)
    earlier = jnp.cumsum(onehot, axis=0) - onehot
    ranked = jnp.sum(earlier * onehot, axis=1)
    return (flat_ids * capacity + ranked).astype(jnp.int32)


def swiglu_back(gate_sum, up_sum, back_sum, weights):
    squash = jax.nn.sigmoid(gate_sum)
    gated_act = gate_sum * squash
    grad_hidden = back_sum * weights.astype(jnp.float32)[:, None]
    grad_up = (grad_hidden * gated_act).astype(jnp.bfloat16)
    grad_gate = (grad_hidden * up_sum * squash * (1.0 + gate_sum * (1.0 - squash))).astype(jnp.bfloat16)
    prob_part = jnp.sum(gated_act * up_sum * back_sum, axis=1)
    return grad_gate, grad_up, prob_part


def reference(tokens, grad_out, route_prob, route_expert, w_gate, w_up, w_down):
    positions = jax.vmap(lambda block_routes: route_slots(block_routes, EXPERTS, CAP))(route_expert.reshape(N_NODE, TOK_NODE * TOPK))
    token_ids = (jnp.arange(TOK_NODE * TOPK, dtype=jnp.int32) // TOPK)[None, :] + (jnp.arange(N_NODE, dtype=jnp.int32) * TOK_NODE)[:, None]
    expert_of = positions // CAP
    slot_of = positions % CAP
    node_of = jnp.broadcast_to(jnp.arange(N_NODE, dtype=jnp.int32)[:, None], positions.shape)
    source_row = jnp.full((EXPERTS, N_NODE, CAP), TOKENS, jnp.int32).at[expert_of, node_of, slot_of].set(token_ids)
    slot_probs = jnp.zeros((EXPERTS, N_NODE, CAP), jnp.bfloat16).at[expert_of, node_of, slot_of].set(route_prob.reshape(N_NODE, TOK_NODE * TOPK))
    padded_tokens = jnp.concatenate([tokens, jnp.zeros((1, D), tokens.dtype)], axis=0)
    padded_grads = jnp.concatenate([grad_out, jnp.zeros((1, D), grad_out.dtype)], axis=0)

    def one_expert(operands):
        rows_e, prob_e, gate_weight, up_weight, down_weight = operands
        row_ids = rows_e.reshape(-1)
        slot_rows = padded_tokens[row_ids]
        slot_grads = padded_grads[row_ids]
        gate_sum = jnp.dot(slot_rows, gate_weight, preferred_element_type=jnp.float32)
        up_sum = jnp.dot(slot_rows, up_weight, preferred_element_type=jnp.float32)
        back_sum = lax.dot_general(slot_grads, down_weight, (((1,), (1,)), ((), ())), preferred_element_type=jnp.float32)
        grad_gate, grad_up, prob_part = swiglu_back(gate_sum, up_sum, back_sum, prob_e.reshape(-1))
        slot_dx = lax.dot_general(grad_gate, gate_weight, (((1,), (1,)), ((), ())), preferred_element_type=jnp.float32)
        slot_dx = slot_dx + lax.dot_general(grad_up, up_weight, (((1,), (1,)), ((), ())), preferred_element_type=jnp.float32)
        return slot_dx.astype(jnp.bfloat16), prob_part.astype(jnp.bfloat16)

    slot_dx, prob_grad = lax.map(one_expert, (source_row, slot_probs, w_gate, w_up, w_down))
    flat_index = (expert_of * (N_NODE * CAP) + node_of * CAP + slot_of).reshape(-1)
    picked = slot_dx.reshape(EXPERTS * N_NODE * CAP, D)[flat_index].astype(jnp.float32)
    grad_tokens = jnp.sum(picked.reshape(TOKENS, TOPK, D), axis=1).astype(jnp.bfloat16)
    grad_prob = prob_grad.reshape(-1)[flat_index].reshape(TOKENS, TOPK)
    return grad_tokens, grad_prob
```

```python
import functools
import jax
import jax.numpy as jnp
from jax import lax
from jax.experimental import pallas as pl
from jax.experimental.pallas import tpu as pltpu
from jax.sharding import PartitionSpec as P

CAP = 4
MESH = pl.DeviceIdType.MESH
LANES = 128
PROB_ROWS = 16


def layout(columns):
    wide = -(-(columns + 1) // LANES) * LANES
    return columns, wide


def expert_kernel(
    n, x_ref, wg_ref, wu_ref, wd_ref, out_ref, start, land, ag, acc, rs_send, rs_recv, ag_send, ag_recv
):
    me = lax.axis_index("local")
    half_ring = n // 2
    slots = x_ref.shape[0]
    rows = slots // 2
    columns, wide = layout(wg_ref.shape[0])
    chunk = wg_ref.shape[1] // n
    to = (lax.rem(me + 1, n), lax.rem(me + n - 1, n))

    def wrap(c):
        return lax.rem(c + 2 * n, n)

    barrier = pltpu.get_barrier_semaphore()
    for neighbour in to:
        pl.semaphore_signal(barrier, inc=1, device_id={"local": neighbour}, device_id_type=MESH)
    pl.semaphore_wait(barrier, 2)

    def span(c):
        return pl.ds(pl.multiple_of(c * chunk, chunk), chunk)

    def term(m, h, c):
        own = pl.ds(h * rows, rows)
        if m == 2:
            return lax.dot_general(
                x_ref[own, wide : wide + columns],
                wd_ref[span(c), :],
                (((1,), (1,)), ((), ())),
                preferred_element_type=jnp.float32,
            )
        weight = wg_ref if m == 0 else wu_ref
        return jnp.dot(x_ref[own, 0:columns], weight[:, span(c)], preferred_element_type=jnp.float32)

    def rs_copy(d, s, h, m, source):
        return pltpu.make_async_remote_copy(
            src_ref=source,
            dst_ref=land.at[d, s, h, m],
            send_sem=rs_send.at[d, s, h, m],
            recv_sem=rs_recv.at[d, s, h, m],
            device_id={"local": to[d]},
            device_id_type=MESH,
        )

    def rs_step(s, fresh, carried):
        chunk_of = (wrap(me + half_ring - s), wrap(me - half_ring + s))
        for h in range(2):
            for m in range(3):
                for d in range(2):
                    if (d, h) in fresh:
                        start[d, h, m] = term(m, h, chunk_of[d]).astype(jnp.bfloat16)
                        rs_copy(d, s, h, m, start.at[d, h, m]).start()
                    elif (d, h) in carried:
                        own = term(m, h, chunk_of[d])
                        held = land.at[d, s - 1, h, m]
                        rs_copy(d, s - 1, h, m, held).wait_recv()
                        held[...] = (own + held[...].astype(jnp.float32)).astype(jnp.bfloat16)
                        rs_copy(d, s, h, m, held).start()

    longer = ((0, 0), (1, 1))
    shorter = ((0, 1), (1, 0))
    rs_step(0, longer, ())
    rs_step(1, shorter, longer)

    def rs_body(s, carry):
        rs_step(s, (), longer + shorter)
        return carry

    lax.fori_loop(2, half_ring, rs_body, 0)

    def ag_copy(d, t, h, part):
        c = wrap(me - t) if d == 0 else wrap(me + t)
        block = ag.at[c, h, pl.ds(0, rows)] if part == 0 else ag.at[c, h, pl.ds(rows, rows + PROB_ROWS)]
        return pltpu.make_async_remote_copy(
            src_ref=block,
            dst_ref=block,
            send_sem=ag_send.at[d, t, h, part],
            recv_sem=ag_recv.at[d, t, h, part],
            device_id={"local": to[d]},
            device_id_type=MESH,
        )

    def ag_wait(d, t, h, part):
        c = wrap(me - 1 - t) if d == 0 else wrap(me + 1 + t)
        block = ag.at[c, h, pl.ds(0, rows)] if part == 0 else ag.at[c, h, pl.ds(rows, rows + PROB_ROWS)]
        pltpu.make_async_remote_copy(
            src_ref=block,
            dst_ref=block,
            send_sem=ag_send.at[d, t, h, part],
            recv_sem=ag_recv.at[d, t, h, part],
            device_id={"local": to[d]},
            device_id_type=MESH,
        ).wait_recv()
        return c

    def product(c, h):
        dims = (((1,), (1,)), ((), ()))
        return lax.dot_general(
            ag[c, h, 0:rows], wg_ref[:, span(c)], dims, preferred_element_type=jnp.float32
        ) + lax.dot_general(
            ag[c, h, rows : 2 * rows], wu_ref[:, span(c)], dims, preferred_element_type=jnp.float32
        )

    last = half_ring - 1
    for h in range(2):
        sums = []
        for m in range(3):
            total = term(m, h, me)
            for d in range(2):
                rs_copy(d, last, h, m, land.at[d, last, h, m]).wait_recv()
                total = total + land[d, last, h, m].astype(jnp.float32)
            sums.append(total)
        gate, up, back = sums
        prob = x_ref[pl.ds(h * rows, rows), columns : columns + 1].astype(jnp.float32)
        squash = jax.nn.sigmoid(gate)
        gated = gate * squash
        hidden = back * prob
        ag[me, h, 0:rows] = (hidden * up * squash * (1.0 + gate * (1.0 - squash))).astype(jnp.bfloat16)
        for d in range(2):
            ag_copy(d, 0, h, 0).start()
        ag[me, h, rows : 2 * rows] = (hidden * gated).astype(jnp.bfloat16)
        both = gated * up * back
        high = both.astype(jnp.bfloat16)
        low = (both - high.astype(jnp.float32)).astype(jnp.bfloat16)
        ones = jnp.ones((8, chunk), jnp.bfloat16)
        dims = (((1,), (1,)), ((), ()))
        part = lax.dot_general(ones, high, dims, preferred_element_type=jnp.float32) + lax.dot_general(
            ones, low, dims, preferred_element_type=jnp.float32
        )
        part_high = part.astype(jnp.bfloat16).astype(jnp.float32)
        both_parts = jnp.concatenate([part_high, part - part_high], axis=0).astype(jnp.bfloat16)
        ag[me, h, 2 * rows : 2 * rows + PROB_ROWS] = both_parts
        for d in range(2):
            ag_copy(d, 0, h, 1).start()
    for h in range(2):
        acc[h] = product(me, h)

    def ag_step(t, forwarded, received):
        for h in range(2):
            came = []
            for part in range(2):
                for d in range(2):
                    if (d, h) in received:
                        c = ag_wait(d, t - 1, h, part)
                        if part == 1:
                            came.append(c)
                    if (d, h) in forwarded:
                        ag_copy(d, t, h, part).start()
            total = acc[h]
            for c in came:
                total = total + product(c, h)
            acc[h] = total

    def ag_body(t, carry):
        ag_step(t, longer + shorter, longer + shorter)
        return carry

    lax.fori_loop(1, half_ring - 1, ag_body, 0)
    ag_step(half_ring - 1, longer, longer + shorter)
    ag_step(half_ring, (), longer)

    for h in range(2):
        parts = jnp.sum(ag[:, h, 2 * rows : 2 * rows + PROB_ROWS].astype(jnp.float32), axis=0)
        whole = parts[0:8] + parts[8:16]
        spread = jnp.transpose(jnp.broadcast_to(whole[0:1], (LANES, rows)))
        out_ref[pl.ds(h * rows, rows), 0:columns] = acc[h].astype(jnp.bfloat16)
        out_ref[pl.ds(h * rows, rows), columns:wide] = spread[:, columns % LANES :].astype(jnp.bfloat16)

    def drain_rs(s, pairs):
        for d, h in pairs:
            for m in range(3):
                rs_copy(d, s, h, m, land.at[d, s, h, m]).wait_send()

    def drain_ag(t, pairs):
        for d, h in pairs:
            for part in range(2):
                ag_copy(d, t, h, part).wait_send()

    drain_rs(0, longer)

    def drain_body(s, carry):
        drain_rs(s, longer + shorter)
        drain_ag(s - 1, longer + shorter)
        return carry

    lax.fori_loop(1, half_ring, drain_body, 0)
    drain_ag(half_ring - 1, longer)


def expert(x, w_gate, w_up, w_down):
    n = lax.axis_size("local")
    slots = x.shape[0]
    columns, wide = layout(w_gate.shape[0])
    rows, chunk, half_ring = slots // 2, w_gate.shape[1] // n, n // 2
    vmem = pl.BlockSpec(memory_space=pltpu.VMEM)
    return pl.pallas_call(
        functools.partial(expert_kernel, n),
        out_shape=jax.ShapeDtypeStruct((slots, wide), jnp.bfloat16),
        in_specs=[vmem] * 4,
        out_specs=vmem,
        scratch_shapes=[
            pltpu.VMEM((2, 2, 3, rows, chunk), jnp.bfloat16),
            pltpu.VMEM((2, half_ring, 2, 3, rows, chunk), jnp.bfloat16),
            pltpu.VMEM((n, 2, 2 * rows + PROB_ROWS, chunk), jnp.bfloat16),
            pltpu.VMEM((2, rows, columns), jnp.float32),
            pltpu.SemaphoreType.DMA((2, half_ring, 2, 3)),
            pltpu.SemaphoreType.DMA((2, half_ring, 2, 3)),
            pltpu.SemaphoreType.DMA((2, half_ring, 2, 2)),
            pltpu.SemaphoreType.DMA((2, half_ring, 2, 2)),
        ],
        compiler_params=pltpu.CompilerParams(
            collective_id=0, has_side_effects=True, vmem_limit_bytes=40 * 1024 * 1024
        ),
    )(x, w_gate, w_up, w_down)


def on_device(tokens, grad_out, route_prob, route_expert, w_gate, w_up, w_down):
    node_count = lax.axis_size("node")
    node_tokens, top_count = route_expert.shape
    columns, wide = layout(tokens.shape[1])
    slots = node_count * CAP
    lane = jnp.arange(slots, dtype=jnp.int32)[None, :]
    named = [route_expert[:, k : k + 1] == lane // CAP for k in range(top_count)]
    hits = functools.reduce(jnp.logical_or, named).astype(jnp.bfloat16)
    order = jnp.arange(node_tokens, dtype=jnp.int32)
    earlier = (order[None, :] < order[:, None]).astype(jnp.bfloat16)
    rank = jnp.dot(earlier, hits, preferred_element_type=jnp.float32)
    fits = rank == (lane % CAP).astype(jnp.float32)
    place = jnp.concatenate([(one & fits) for one in named], axis=0).astype(jnp.bfloat16)
    blank = jnp.zeros((node_tokens, wide - columns - 1), jnp.bfloat16)
    blank_wide = jnp.zeros((node_tokens, wide - columns), jnp.bfloat16)
    source = jnp.concatenate(
        [
            jnp.concatenate([tokens, route_prob[:, k : k + 1], blank, grad_out, blank_wide], axis=1)
            for k in range(top_count)
        ],
        axis=0,
    )
    send = lax.dot_general(
        place, source, (((0,), (0,)), ((), ())), preferred_element_type=jnp.float32
    ).astype(jnp.bfloat16)
    arrived = lax.all_to_all(
        send.reshape(node_count, CAP, 2 * wide), "node", split_axis=0, concat_axis=0, tiled=True
    ).reshape(slots, 2 * wide)
    result = expert(arrived, w_gate[0], w_up[0], w_down[0])
    returned = lax.all_to_all(
        result.reshape(node_count, CAP, wide), "node", split_axis=0, concat_axis=0, tiled=True
    ).reshape(slots, wide)
    picked = jnp.dot(place, returned, preferred_element_type=jnp.float32).reshape(
        top_count, node_tokens, wide
    )
    grad_tokens = jnp.sum(picked[:, :, 0:columns], axis=0).astype(jnp.bfloat16)
    grad_prob = picked[:, :, columns].T.astype(jnp.bfloat16)
    return grad_tokens, grad_prob


def solution(mesh):
    return jax.shard_map(
        on_device,
        mesh=mesh,
        in_specs=(
            P("node", "local"),
            P("node", "local"),
            P("node", None),
            P("node", None),
            P("node", "local", None),
            P("node", "local", None),
            P("node", None, "local"),
        ),
        out_specs=(P("node", "local"), P("node", None)),
        check_vma=False,
    )
```

```python
import functools
import jax
import jax.numpy as jnp
from jax import lax
from jax.experimental import pallas as pl
from jax.experimental.pallas import tpu as pltpu
from jax.sharding import PartitionSpec as P

CAP = 4
MESH = pl.DeviceIdType.MESH
LANES = 128
BF16, F32 = jnp.bfloat16, jnp.float32
CROSS = (((1,), (1,)), ((), ()))


def iota(shape, dim):
    return lax.broadcasted_iota(jnp.int32, shape, dim)


def ones_where(mask):
    return jnp.where(mask, 1.0, 0.0).astype(BF16)


def mult(a, b):
    return jnp.dot(a, b, preferred_element_type=F32)


def moe_kernel(
    nodes, n, tok_ref, grad_ref, prob_ref, route_ref, wg_hbm, wu_hbm, wd_hbm, dx_ref, dp_ref,
    wg, wu, wd, outbox, inbox, xs, terms, start, land, ag, pp, acc, outbox2, inbox2,
    w_sem, out_send, out_recv, rs_send, rs_recv, ag_send, ag_recv, back_send, back_recv,
):
    node, me = lax.axis_index("node"), lax.axis_index("local")
    half_ring = n // 2
    slots = nodes * CAP
    rows = slots // 2
    piece = rows // 2
    columns = tok_ref.shape[1]
    rest = columns - LANES
    top, tokens = route_ref.shape
    pairs = top * tokens
    chunk = wg.shape[1] // n
    to = (lax.rem(me + 1, n), lax.rem(me + n - 1, n))

    loads = [
        pltpu.make_async_copy(source, kept, w_sem.at[i])
        for i, (source, kept) in enumerate(((wg_hbm, wg), (wu_hbm, wu), (wd_hbm, wd)))
    ]
    for load in loads:
        load.start()

    barrier = pltpu.get_barrier_semaphore()

    def greet(i, carry):
        pl.semaphore_signal(
            barrier, inc=1, device_id={"node": lax.rem(node + i, nodes)}, device_id_type=MESH
        )
        return carry

    lax.fori_loop(1, nodes, greet, 0)
    for neighbour in to:
        pl.semaphore_signal(barrier, inc=1, device_id={"local": neighbour}, device_id_type=MESH)

    def flat(ref):
        kept = ref[...].astype(F32)
        return jnp.concatenate([kept[k : k + 1] for k in range(top)], axis=1)

    diagonal = iota((pairs, pairs), 0) == iota((pairs, pairs), 1)

    def upright(row):
        return jnp.sum(jnp.where(diagonal, row, 0.0), axis=1, keepdims=True)

    expert_row = flat(route_ref)
    expert_col = upright(expert_row)
    same = expert_row == expert_col
    token_down, token_along = iota((pairs, pairs), 0) % tokens, iota((pairs, pairs), 1) % tokens
    rank_row = jnp.sum(jnp.where(same & (token_down < token_along), 1.0, 0.0), axis=0, keepdims=True)
    rank_col = jnp.sum(jnp.where(same & (token_along < token_down), 1.0, 0.0), axis=1, keepdims=True)
    prob_col = upright(flat(prob_ref))

    blank = jnp.zeros((tokens, LANES - rest), F32)
    lane = iota((pairs, LANES), 1)

    def stacked(block):
        return jnp.concatenate([block] * top, axis=0)

    held_tokens, held_grads = tok_ref[...].astype(F32), grad_ref[...].astype(F32)
    source = jnp.concatenate(
        [
            stacked(held_tokens[:, 0:LANES]),
            jnp.where(
                lane == rest,
                prob_col,
                stacked(jnp.concatenate([held_tokens[:, LANES:columns], blank], axis=1)),
            ),
            stacked(held_grads[:, 0:LANES]),
            stacked(jnp.concatenate([held_grads[:, LANES:columns], blank], axis=1)),
        ],
        axis=0,
    ).astype(BF16)
    target = (expert_row * (4 * CAP) + rank_row).astype(jnp.int32)
    targets = jnp.concatenate([target + CAP * j for j in range(4)], axis=1)
    place = ones_where(iota((4 * slots, 4 * pairs), 0) == targets)
    outbox[...] = mult(place, source).astype(BF16).reshape(outbox.shape)
    inbox[node] = outbox[node]

    pl.semaphore_wait(barrier, nodes + 1)

    def send_copy(peer):
        return pltpu.make_async_remote_copy(
            src_ref=outbox.at[peer],
            dst_ref=inbox.at[node],
            send_sem=out_send,
            recv_sem=out_recv,
            device_id={"node": peer},
            device_id_type=MESH,
        )

    def send_body(i, carry):
        send_copy(lax.rem(node + i, nodes)).start()
        return carry

    lax.fori_loop(1, nodes, send_body, 0)

    group = 64 // CAP
    down, along = iota((256, 256), 0), iota((256, 256), 1)
    sender, rest_of = along // (4 * CAP), along % (4 * CAP)
    order_in = ones_where(down == 64 * (rest_of // CAP) + CAP * sender + rest_of % CAP)
    sender2, rest_of2 = down // (2 * CAP), down % (2 * CAP)
    order_out = ones_where(along == rows * (rest_of2 // CAP) + CAP * sender2 + rest_of2 % CAP)
    target2 = (expert_col * (2 * CAP) + rank_col).astype(jnp.int32)
    targets2 = jnp.concatenate([target2, target2 + CAP], axis=0)
    pick = ones_where(iota((2 * pairs, 2 * slots), 1) == targets2)

    for load in loads:
        load.wait()

    def all_of(send, recv, source, into):
        return pltpu.make_async_remote_copy(
            src_ref=source.at[pl.ds(0, nodes - 1)],
            dst_ref=into.at[pl.ds(0, nodes - 1)],
            send_sem=send,
            recv_sem=recv,
            device_id={"node": lax.rem(node + 1, nodes)},
            device_id_type=MESH,
        )

    all_of(out_send, out_recv, outbox, inbox).wait_recv()
    arrived = inbox[...].reshape(4 * slots, LANES)
    blocks = slots // 64
    mixed = mult(
        order_in, jnp.concatenate([arrived[256 * g : 256 * g + 256] for g in range(blocks)], axis=1)
    ).astype(BF16)
    for g in range(blocks):
        for j in range(4):
            xs[64 * g : 64 * g + 64, LANES * j : LANES * (j + 1)] = mixed[
                64 * j : 64 * j + 64, LANES * g : LANES * (g + 1)
            ]

    def wrap(c):
        return lax.rem(c + 2 * n, n)

    def span(c):
        return pl.ds(pl.multiple_of(c * chunk, chunk), chunk)

    def term(m, c):
        if m == 2:
            return mult(xs[:, 2 * LANES : 2 * LANES + columns], wd[:, span(c)])
        return mult(xs[:, 0:columns], (wg, wu)[m][:, span(c)])

    def own_rows(h):
        return pl.ds(h * rows, rows)

    def rs_copy(d, s, h, m, source):
        return pltpu.make_async_remote_copy(
            src_ref=source,
            dst_ref=land.at[d, s, h, m],
            send_sem=rs_send.at[d, s, h, m],
            recv_sem=rs_recv.at[d, s, h, m],
            device_id={"local": to[d]},
            device_id_type=MESH,
        )

    def chunks_at(s):
        return (wrap(me + half_ring - s), wrap(me - half_ring + s))

    def terms_for(s):
        for d, c in enumerate(chunks_at(s)):
            for m in range(3):
                terms[d, m] = term(m, c)

    longer = ((0, 0), (1, 1))
    shorter = ((0, 1), (1, 0))

    def rs_step(s, fresh):
        for h in range(2):
            for m in range(3):
                for d in range(2):
                    own = terms[d, m, own_rows(h)]
                    if (d, h) in fresh:
                        start[d, h, m] = own.astype(BF16)
                        rs_copy(d, s, h, m, start.at[d, h, m]).start()
                    else:
                        held = land.at[d, s - 1, h, m]
                        rs_copy(d, s - 1, h, m, held).wait_recv()
                        held[...] = (own + held[...].astype(F32)).astype(BF16)
                        rs_copy(d, s, h, m, held).start()

    for m in range(3):
        both = term(m, wrap(me + half_ring))
        for d, h in longer:
            start[d, h, m] = both[h * rows : (h + 1) * rows].astype(BF16)
            rs_copy(d, 0, h, m, start.at[d, h, m]).start()
    terms_for(1)
    rs_step(1, shorter)

    def rs_body(s, carry):
        terms_for(s)
        rs_step(s, ())
        return carry

    lax.fori_loop(2, half_ring, rs_body, 0)
    for m in range(3):
        terms[0, m] = term(m, me)

    order = (0, 1, 4, 2, 3)

    def is_longer(d, q):
        return d == (0 if q < 2 else 1)

    def ag_copy(d, t, q, c):
        block = pp.at[c] if q == 4 else ag.at[c, pl.ds(q * piece, piece)]
        return pltpu.make_async_remote_copy(
            src_ref=block,
            dst_ref=block,
            send_sem=ag_send.at[d, t, q],
            recv_sem=ag_recv.at[d, t, q],
            device_id={"local": to[d]},
            device_id_type=MESH,
        )

    def sent_at(d, t):
        return wrap(me - t) if d == 0 else wrap(me + t)

    def ag_wait(d, t, q):
        ag_copy(d, t, q, sent_at(d, t + 1)).wait_recv()

    def product(c, first, count):
        weights = jnp.concatenate([wg[:, span(c)], wu[:, span(c)]], axis=1)
        return lax.dot_general(
            ag[c, pl.ds(first, count)], weights, CROSS, preferred_element_type=F32
        )

    last = half_ring - 1
    for h in range(2):
        sums = []
        for m in range(3):
            total = terms[0, m, own_rows(h)]
            for d in range(2):
                rs_copy(d, last, h, m, land.at[d, last, h, m]).wait_recv()
                total = total + land[d, last, h, m].astype(F32)
            sums.append(total)
        gate, up, back = sums
        prob = xs[own_rows(h), columns : columns + 1].astype(F32)
        squash = jax.nn.sigmoid(gate)
        gated = gate * squash
        hidden = back * prob
        ag[me, own_rows(h), 0:chunk] = (
            hidden * up * squash * (1.0 + gate * (1.0 - squash))
        ).astype(BF16)
        ag[me, own_rows(h), chunk : 2 * chunk] = (hidden * gated).astype(BF16)
        if h == 0:
            for q in (0, 1):
                for d in range(2):
                    ag_copy(d, 0, q, me).start()
        both = gated * up * back
        high = both.astype(BF16)
        low = (both - high.astype(F32)).astype(BF16)
        ones = jnp.ones((8, chunk), BF16)
        part = lax.dot_general(ones, high, CROSS, preferred_element_type=F32) + lax.dot_general(
            ones, low, CROSS, preferred_element_type=F32
        )
        pp[me, 4 * h : 4 * h + 4] = part[0:4]
    for q in (4, 2, 3):
        for d in range(2):
            ag_copy(d, 0, q, me).start()
    acc[...] = product(me, 0, slots)

    def ag_step(t, all_forwarded):
        for q in order:
            for d in range(2):
                ag_wait(d, t - 1, q)
                if all_forwarded or is_longer(d, q):
                    ag_copy(d, t, q, sent_at(d, t)).start()
        acc[...] += product(sent_at(0, t), 0, slots) + product(sent_at(1, t), 0, slots)

    def ag_body(t, carry):
        ag_step(t, True)
        return carry

    lax.fori_loop(1, half_ring - 1, ag_body, 0)
    ag_step(half_ring - 1, False)

    def back_copy(peer):
        return pltpu.make_async_remote_copy(
            src_ref=outbox2.at[peer],
            dst_ref=inbox2.at[node],
            send_sem=back_send,
            recv_sem=back_recv,
            device_id={"node": peer},
            device_id_type=MESH,
        )

    farthest = wrap(me + half_ring)
    for h in range(2):
        for q in (2 * h, 2 * h + 1):
            ag_wait(h, last, q)
        total = acc[own_rows(h)] + product(farthest, h * rows, rows)
        if h == 0:
            ag_wait(1, last, 4)
            weight_sums = jnp.sum(pp[...], axis=0)
        spread = jnp.transpose(jnp.broadcast_to(weight_sums[4 * h : 4 * h + 1], (LANES, rows)))
        stack = jnp.concatenate(
            [
                total[:, 0:LANES],
                jnp.concatenate([total[:, LANES:columns], spread[:, rest:LANES]], axis=1),
            ],
            axis=0,
        ).astype(BF16)
        half = nodes // 2
        outbox2[h * half : (h + 1) * half] = (
            mult(order_out, stack).reshape((half,) + outbox2.shape[1:]).astype(BF16)
        )

        def back_body(i, carry, h=h, half=half):
            peer = h * half + lax.rem(node + i, half)

            @pl.when(peer != node)
            def _():
                back_copy(peer).start()

            return carry

        lax.fori_loop(0, half, back_body, 0)
    inbox2[node] = outbox2[node]

    all_of(back_send, back_recv, outbox2, inbox2).wait_recv()
    returned = inbox2[...].astype(F32).reshape(2 * slots, LANES).astype(BF16)
    picked = mult(pick, returned)
    low_sum, high_sum = picked[0:tokens], picked[pairs : pairs + tokens]
    for k in range(1, top):
        low_sum += picked[k * tokens : (k + 1) * tokens]
        high_sum += picked[pairs + k * tokens : pairs + (k + 1) * tokens]
    dx_ref[:, 0:LANES] = low_sum.astype(BF16)
    dx_ref[:, LANES:columns] = high_sum[:, 0:rest].astype(BF16)
    prob_grad = picked[pairs : 2 * pairs, rest : rest + 1]
    along_row = jnp.sum(jnp.where(diagonal, prob_grad, 0.0), axis=0, keepdims=True)
    dp_ref[...] = jnp.concatenate(
        [along_row[:, k * tokens : (k + 1) * tokens] for k in range(top)], axis=0
    ).astype(BF16)

    all_of(out_send, out_recv, outbox, inbox).wait_send()
    all_of(back_send, back_recv, outbox2, inbox2).wait_send()

    def drain(s, rs_streams, ag_all):
        for d, h in rs_streams:
            for m in range(3):
                rs_copy(d, s, h, m, land.at[d, s, h, m]).wait_send()
        for q in order:
            for d in range(2):
                if ag_all or is_longer(d, q):
                    ag_copy(d, s, q, me).wait_send()

    drain(0, longer, True)

    def drain_body(s, carry):
        drain(s, longer + shorter, True)
        return carry

    lax.fori_loop(1, half_ring - 1, drain_body, 0)
    drain(half_ring - 1, longer + shorter, False)


def on_device(tokens, grad_out, route_prob, route_expert, w_gate, w_up, w_down):
    nodes, n = lax.axis_size("node"), lax.axis_size("local")
    slots = nodes * CAP
    width, hidden = w_gate.shape[1:]
    rows, chunk, half_ring = slots // 2, hidden // n, n // 2
    vmem, hbm = pl.BlockSpec(memory_space=pltpu.VMEM), pl.BlockSpec(memory_space=pl.ANY)
    block_tokens, top = route_expert.shape
    dma = pltpu.SemaphoreType.DMA
    grad_tokens, grad_prob = pl.pallas_call(
        functools.partial(moe_kernel, nodes, n),
        out_shape=(
            jax.ShapeDtypeStruct(tokens.shape, BF16),
            jax.ShapeDtypeStruct((top, block_tokens), BF16),
        ),
        in_specs=[vmem] * 4 + [hbm] * 3,
        out_specs=(vmem, vmem),
        scratch_shapes=[
            pltpu.VMEM((width, hidden), BF16),
            pltpu.VMEM((width, hidden), BF16),
            pltpu.VMEM((width, hidden), BF16),
            pltpu.VMEM((nodes, 4 * CAP, LANES), BF16),
            pltpu.VMEM((nodes, 4 * CAP, LANES), BF16),
            pltpu.VMEM((slots, 4 * LANES), BF16),
            pltpu.VMEM((2, 3, slots, chunk), F32),
            pltpu.VMEM((2, 2, 3, rows, chunk), BF16),
            pltpu.VMEM((2, half_ring, 2, 3, rows, chunk), BF16),
            pltpu.VMEM((n, slots, 2 * chunk), BF16),
            pltpu.VMEM((n, 8, LANES), F32),
            pltpu.VMEM((slots, width), F32),
            pltpu.VMEM((nodes, 2 * CAP, LANES), BF16),
            pltpu.VMEM((nodes, 2 * CAP, LANES), BF16),
            dma((3,)),
            dma,
            dma,
            dma((2, half_ring, 2, 3)),
            dma((2, half_ring, 2, 3)),
            dma((2, half_ring, 5)),
            dma((2, half_ring, 5)),
            dma,
            dma,
        ],
        compiler_params=pltpu.CompilerParams(
            collective_id=0, has_side_effects=True, vmem_limit_bytes=56 * 1024 * 1024
        ),
    )(
        tokens,
        grad_out,
        route_prob.T,
        route_expert.T,
        w_gate[0],
        w_up[0],
        jnp.swapaxes(w_down[0], 0, 1),
    )
    return grad_tokens, grad_prob.T


def solution(mesh):
    return jax.shard_map(
        on_device,
        mesh=mesh,
        in_specs=(
            P("node", "local"),
            P("node", "local"),
            P("node", None),
            P("node", None),
            P("node", "local", None),
            P("node", "local", None),
            P("node", None, "local"),
        ),
        out_specs=(P("node", "local"), P("node", None)),
        check_vma=False,
    )
```

```python
import functools
import jax
import jax.numpy as jnp
from jax import lax
from jax.experimental import pallas as pl
from jax.experimental.pallas import tpu as pltpu
from jax.sharding import PartitionSpec as P

CAP = 4
MESH = pl.DeviceIdType.MESH
LANES = 128
BF16, F32 = jnp.bfloat16, jnp.float32
CROSS = (((1,), (1,)), ((), ()))


def iota(shape, dim):
    return lax.broadcasted_iota(jnp.int32, shape, dim)


def ones_where(mask):
    return jnp.where(mask, 1.0, 0.0).astype(BF16)


def mult(a, b):
    return jnp.dot(a, b, preferred_element_type=F32)


def moe_kernel(
    nodes, n, tok_ref, grad_ref, prob_ref, route_ref, wg_hbm, wu_hbm, wd_hbm, dx_ref, dp_ref,
    wg, wu, wd, outbox, inbox, xs, terms, start, land, ag, pp, acc, outbox2, inbox2,
    w_sem, out_send, out_recv, rs_send, rs_recv, ag_send, ag_recv, back_send, back_recv,
):
    node, me = lax.axis_index("node"), lax.axis_index("local")
    half_ring = n // 2
    slots = nodes * CAP
    rows = slots // 2
    piece = rows // 2
    columns = tok_ref.shape[1]
    rest = columns - LANES
    top, tokens = route_ref.shape
    pairs = top * tokens
    chunk = wg.shape[1] // n
    to = (lax.rem(me + 1, n), lax.rem(me + n - 1, n))

    loads = [
        pltpu.make_async_copy(source, kept, w_sem.at[i])
        for i, (source, kept) in enumerate(((wg_hbm, wg), (wu_hbm, wu), (wd_hbm, wd)))
    ]
    for load in loads:
        load.start()

    barrier = pltpu.get_barrier_semaphore()

    def greet(i, carry):
        pl.semaphore_signal(
            barrier, inc=1, device_id={"node": lax.rem(node + i, nodes)}, device_id_type=MESH
        )
        return carry

    lax.fori_loop(1, nodes, greet, 0)
    for neighbour in to:
        pl.semaphore_signal(barrier, inc=1, device_id={"local": neighbour}, device_id_type=MESH)

    def flat(ref):
        kept = ref[...].astype(F32)
        return jnp.concatenate([kept[k : k + 1] for k in range(top)], axis=1)

    diagonal = iota((pairs, pairs), 0) == iota((pairs, pairs), 1)

    def upright(row):
        return jnp.sum(jnp.where(diagonal, row, 0.0), axis=1, keepdims=True)

    expert_row = flat(route_ref)
    expert_col = upright(expert_row)
    same = expert_row == expert_col
    token_down, token_along = iota((pairs, pairs), 0) % tokens, iota((pairs, pairs), 1) % tokens
    rank_row = jnp.sum(jnp.where(same & (token_down < token_along), 1.0, 0.0), axis=0, keepdims=True)
    rank_col = jnp.sum(jnp.where(same & (token_along < token_down), 1.0, 0.0), axis=1, keepdims=True)
    prob_col = upright(flat(prob_ref))

    blank = jnp.zeros((tokens, LANES - rest), F32)
    lane = iota((pairs, LANES), 1)

    def stacked(block):
        return jnp.concatenate([block] * top, axis=0)

    held_tokens, held_grads = tok_ref[...].astype(F32), grad_ref[...].astype(F32)
    first_blocks = jnp.concatenate([held_tokens[:, 0:LANES], held_grads[:, 0:LANES]], axis=1)
    token_block = jnp.where(
        lane == rest,
        prob_col,
        stacked(jnp.concatenate([held_tokens[:, LANES:columns], blank], axis=1)),
    )
    grad_block = stacked(jnp.concatenate([held_grads[:, LANES:columns], blank], axis=1))
    source = jnp.concatenate(
        [stacked(first_blocks), jnp.concatenate([token_block, grad_block], axis=1)], axis=0
    ).astype(BF16)
    target = (expert_row * (2 * CAP) + rank_row).astype(jnp.int32)
    targets = jnp.concatenate([target, target + CAP], axis=1)
    place = ones_where(iota((2 * slots, 2 * pairs), 0) == targets)
    filled = mult(place, source)
    for part in range(2):
        block = filled[:, part * LANES : (part + 1) * LANES]
        outbox[part] = block.reshape(outbox.shape[1:]).astype(BF16)
        inbox[part, node] = outbox[part, node]

    pl.semaphore_wait(barrier, nodes + 1)

    def send_body(part, i):
        peer = lax.rem(node + i, nodes)
        pltpu.make_async_remote_copy(
            src_ref=outbox.at[part, peer],
            dst_ref=inbox.at[part, node],
            send_sem=out_send.at[part],
            recv_sem=out_recv.at[part],
            device_id={"node": peer},
            device_id_type=MESH,
        ).start()

    for part in range(2):

        def send_part(i, carry, part=part):
            send_body(part, i)
            return carry

        lax.fori_loop(1, nodes, send_part, 0)

    down, along = iota((slots, slots), 0), iota((slots, slots), 1)
    sender, rest_of = along // (2 * CAP), along % (2 * CAP)
    order_in = ones_where(down == rows * (rest_of // CAP) + CAP * sender + rest_of % CAP)
    sender2, rest_of2 = down // (2 * CAP), down % (2 * CAP)
    order_out = ones_where(along == rows * (rest_of2 // CAP) + CAP * sender2 + rest_of2 % CAP)
    target2 = (expert_col * (2 * CAP) + rank_col).astype(jnp.int32)
    targets2 = jnp.concatenate([target2, target2 + CAP], axis=0)
    pick = ones_where(iota((2 * pairs, 2 * slots), 1) == targets2)

    for load in loads:
        load.wait()

    def all_of(send, recv, source, into):
        return pltpu.make_async_remote_copy(
            src_ref=source.at[pl.ds(0, nodes - 1)],
            dst_ref=into.at[pl.ds(0, nodes - 1)],
            send_sem=send,
            recv_sem=recv,
            device_id={"node": lax.rem(node + 1, nodes)},
            device_id_type=MESH,
        )

    def all_out(part):
        return all_of(out_send.at[part], out_recv.at[part], outbox.at[part], inbox.at[part])

    def receive(part):
        all_out(part).wait_recv()
        arrived = inbox[part].astype(F32).reshape(2 * slots, LANES).astype(BF16)
        mixed = mult(
            order_in, jnp.concatenate([arrived[0:slots], arrived[slots : 2 * slots]], axis=1)
        ).astype(BF16)
        for g in range(2):
            for j in range(2):
                column = LANES * (2 * part + j)
                xs[g * rows : (g + 1) * rows, column : column + LANES] = mixed[
                    j * rows : (j + 1) * rows, g * LANES : (g + 1) * LANES
                ]

    def wrap(c):
        return lax.rem(c + 2 * n, n)

    def span(c):
        return pl.ds(pl.multiple_of(c * chunk, chunk), chunk)

    def term(m, c):
        if m == 2:
            return mult(xs[:, 2 * LANES : 2 * LANES + columns], wd[:, span(c)])
        return mult(xs[:, 0:columns], (wg, wu)[m][:, span(c)])

    def own_rows(h):
        return pl.ds(h * rows, rows)

    def rs_copy(d, s, h, m, source):
        return pltpu.make_async_remote_copy(
            src_ref=source,
            dst_ref=land.at[d, s, h, m],
            send_sem=rs_send.at[d, s, h, m],
            recv_sem=rs_recv.at[d, s, h, m],
            device_id={"local": to[d]},
            device_id_type=MESH,
        )

    def chunks_at(s):
        return (wrap(me + half_ring - s), wrap(me - half_ring + s))

    def terms_for(s, kinds):
        for d, c in enumerate(chunks_at(s)):
            for m in kinds:
                terms[d, m] = term(m, c)

    longer = ((0, 0), (1, 1))
    shorter = ((0, 1), (1, 0))

    def begin(d, s, h, m, own):
        start[d, h, m] = own.astype(BF16)
        rs_copy(d, s, h, m, start.at[d, h, m]).start()

    def go_on(d, s, h, m):
        held = land.at[d, s - 1, h, m]
        rs_copy(d, s - 1, h, m, held).wait_recv()
        held[...] = (terms[d, m, own_rows(h)] + held[...].astype(F32)).astype(BF16)
        rs_copy(d, s, h, m, held).start()

    for kinds in ((0, 1), (2,)):
        receive(0 if 0 in kinds else 1)
        for m in kinds:
            both = term(m, wrap(me + half_ring))
            for d, h in longer:
                begin(d, 0, h, m, both[h * rows : (h + 1) * rows])
        terms_for(1, kinds)
        for m in kinds:
            for d, h in shorter:
                begin(d, 1, h, m, terms[d, m, own_rows(h)])
    for m in range(3):
        for d, h in longer:
            go_on(d, 1, h, m)

    def rs_body(s, carry):
        terms_for(s, range(3))
        for h in range(2):
            for m in range(3):
                for d in range(2):
                    go_on(d, s, h, m)
        return carry

    lax.fori_loop(2, half_ring, rs_body, 0)
    for m in range(3):
        terms[0, m] = term(m, me)

    order = (0, 1, 4, 2, 3)

    def is_longer(d, q):
        return d == (0 if q < 2 else 1)

    def ag_copy(d, t, q, c):
        block = pp.at[c] if q == 4 else ag.at[c, pl.ds(q * piece, piece)]
        return pltpu.make_async_remote_copy(
            src_ref=block,
            dst_ref=block,
            send_sem=ag_send.at[d, t, q],
            recv_sem=ag_recv.at[d, t, q],
            device_id={"local": to[d]},
            device_id_type=MESH,
        )

    def sent_at(d, t):
        return wrap(me - t) if d == 0 else wrap(me + t)

    def ag_wait(d, t, q):
        ag_copy(d, t, q, sent_at(d, t + 1)).wait_recv()

    def product(c, first, count):
        weights = jnp.concatenate([wg[:, span(c)], wu[:, span(c)]], axis=1)
        return lax.dot_general(
            ag[c, pl.ds(first, count)], weights, CROSS, preferred_element_type=F32
        )

    last = half_ring - 1
    for h in range(2):
        sums = []
        for m in range(3):
            total = terms[0, m, own_rows(h)]
            for d in range(2):
                rs_copy(d, last, h, m, land.at[d, last, h, m]).wait_recv()
                total = total + land[d, last, h, m].astype(F32)
            sums.append(total)
        gate, up, back = sums
        prob = xs[own_rows(h), columns : columns + 1].astype(F32)
        squash = jax.nn.sigmoid(gate)
        gated = gate * squash
        hidden = back * prob
        ag[me, own_rows(h), 0:chunk] = (
            hidden * up * squash * (1.0 + gate * (1.0 - squash))
        ).astype(BF16)
        ag[me, own_rows(h), chunk : 2 * chunk] = (hidden * gated).astype(BF16)
        if h == 0:
            for q in (0, 1):
                for d in range(2):
                    ag_copy(d, 0, q, me).start()
        both = gated * up * back
        high = both.astype(BF16)
        low = (both - high.astype(F32)).astype(BF16)
        ones = jnp.ones((8, chunk), BF16)
        part = lax.dot_general(ones, high, CROSS, preferred_element_type=F32) + lax.dot_general(
            ones, low, CROSS, preferred_element_type=F32
        )
        pp[me, 4 * h : 4 * h + 4] = part[0:4]
    for q in (4, 2, 3):
        for d in range(2):
            ag_copy(d, 0, q, me).start()
    acc[...] = product(me, 0, slots)

    def ag_step(t, all_forwarded):
        for q in order:
            for d in range(2):
                ag_wait(d, t - 1, q)
                if all_forwarded or is_longer(d, q):
                    ag_copy(d, t, q, sent_at(d, t)).start()
        acc[...] += product(sent_at(0, t), 0, slots) + product(sent_at(1, t), 0, slots)

    def ag_body(t, carry):
        ag_step(t, True)
        return carry

    lax.fori_loop(1, half_ring - 1, ag_body, 0)
    ag_step(half_ring - 1, False)

    def back_copy(peer):
        return pltpu.make_async_remote_copy(
            src_ref=outbox2.at[peer],
            dst_ref=inbox2.at[node],
            send_sem=back_send,
            recv_sem=back_recv,
            device_id={"node": peer},
            device_id_type=MESH,
        )

    farthest = wrap(me + half_ring)
    for h in range(2):
        for q in (2 * h, 2 * h + 1):
            ag_wait(h, last, q)
        total = acc[own_rows(h)] + product(farthest, h * rows, rows)
        if h == 0:
            ag_wait(1, last, 4)
            weight_sums = jnp.sum(pp[...], axis=0)
        spread = jnp.transpose(jnp.broadcast_to(weight_sums[4 * h : 4 * h + 1], (LANES, rows)))
        stack = jnp.concatenate(
            [
                total[:, 0:LANES],
                jnp.concatenate([total[:, LANES:columns], spread[:, rest:LANES]], axis=1),
            ],
            axis=0,
        ).astype(BF16)
        half = nodes // 2
        outbox2[h * half : (h + 1) * half] = (
            mult(order_out, stack).reshape((half,) + outbox2.shape[1:]).astype(BF16)
        )

        def back_body(i, carry, h=h, half=half):
            peer = h * half + lax.rem(node + i, half)

            @pl.when(peer != node)
            def _():
                back_copy(peer).start()

            return carry

        lax.fori_loop(0, half, back_body, 0)
    inbox2[node] = outbox2[node]

    def drain(s, rs_streams, ag_all):
        for d, h in rs_streams:
            for m in range(3):
                rs_copy(d, s, h, m, land.at[d, s, h, m]).wait_send()
        for q in order:
            for d in range(2):
                if ag_all or is_longer(d, q):
                    ag_copy(d, s, q, me).wait_send()

    drain(0, longer, True)

    def drain_body(s, carry):
        drain(s, longer + shorter, True)
        return carry

    lax.fori_loop(1, half_ring - 1, drain_body, 0)
    drain(half_ring - 1, longer + shorter, False)
    for part in range(2):
        all_out(part).wait_send()

    all_of(back_send, back_recv, outbox2, inbox2).wait_recv()
    returned = inbox2[...].astype(F32).reshape(2 * slots, LANES).astype(BF16)
    picked = mult(pick, returned)
    low_sum, high_sum = picked[0:tokens], picked[pairs : pairs + tokens]
    for k in range(1, top):
        low_sum += picked[k * tokens : (k + 1) * tokens]
        high_sum += picked[pairs + k * tokens : pairs + (k + 1) * tokens]
    dx_ref[:, 0:LANES] = low_sum
    dx_ref[:, LANES:columns] = high_sum[:, 0:rest]
    prob_grad = picked[pairs : 2 * pairs, rest : rest + 1]
    along_row = jnp.sum(jnp.where(diagonal, prob_grad, 0.0), axis=0, keepdims=True)
    dp_ref[...] = jnp.concatenate(
        [along_row[:, k * tokens : (k + 1) * tokens] for k in range(top)], axis=0
    )

    all_of(back_send, back_recv, outbox2, inbox2).wait_send()


def on_device(tokens, grad_out, route_prob, route_expert, w_gate, w_up, w_down):
    nodes, n = lax.axis_size("node"), lax.axis_size("local")
    slots = nodes * CAP
    width, hidden = w_gate.shape[1:]
    rows, chunk, half_ring = slots // 2, hidden // n, n // 2
    vmem, hbm = pl.BlockSpec(memory_space=pltpu.VMEM), pl.BlockSpec(memory_space=pl.ANY)
    block_tokens, top = route_expert.shape
    dma = pltpu.SemaphoreType.DMA
    grad_tokens, grad_prob = pl.pallas_call(
        functools.partial(moe_kernel, nodes, n),
        out_shape=(
            jax.ShapeDtypeStruct(tokens.shape, F32),
            jax.ShapeDtypeStruct((top, block_tokens), F32),
        ),
        in_specs=[vmem] * 4 + [hbm] * 3,
        out_specs=(vmem, vmem),
        scratch_shapes=[
            pltpu.VMEM((width, hidden), BF16),
            pltpu.VMEM((width, hidden), BF16),
            pltpu.VMEM((width, hidden), BF16),
            pltpu.VMEM((2, nodes, 2 * CAP, LANES), BF16),
            pltpu.VMEM((2, nodes, 2 * CAP, LANES), BF16),
            pltpu.VMEM((slots, 4 * LANES), BF16),
            pltpu.VMEM((2, 3, slots, chunk), F32),
            pltpu.VMEM((2, 2, 3, rows, chunk), BF16),
            pltpu.VMEM((2, half_ring, 2, 3, rows, chunk), BF16),
            pltpu.VMEM((n, slots, 2 * chunk), BF16),
            pltpu.VMEM((n, 8, LANES), F32),
            pltpu.VMEM((slots, width), F32),
            pltpu.VMEM((nodes, 2 * CAP, LANES), BF16),
            pltpu.VMEM((nodes, 2 * CAP, LANES), BF16),
            dma((3,)),
            dma((2,)),
            dma((2,)),
            dma((2, half_ring, 2, 3)),
            dma((2, half_ring, 2, 3)),
            dma((2, half_ring, 5)),
            dma((2, half_ring, 5)),
            dma,
            dma,
        ],
        compiler_params=pltpu.CompilerParams(
            collective_id=0, has_side_effects=True, vmem_limit_bytes=56 * 1024 * 1024
        ),
    )(
        tokens,
        grad_out,
        route_prob.T,
        route_expert.T,
        w_gate[0],
        w_up[0],
        jnp.swapaxes(w_down[0], 0, 1),
    )
    return grad_tokens.astype(BF16), grad_prob.T.astype(BF16)


def solution(mesh):
    return jax.shard_map(
        on_device,
        mesh=mesh,
        in_specs=(
            P("node", "local"),
            P("node", "local"),
            P("node", None),
            P("node", None),
            P("node", "local", None),
            P("node", "local", None),
            P("node", None, "local"),
        ),
        out_specs=(P("node", "local"), P("node", None)),
        check_vma=False,
    )
```

```python
import functools
import jax
import jax.numpy as jnp
from jax import lax
from jax.experimental import pallas as pl
from jax.experimental.pallas import tpu as pltpu
from jax.sharding import PartitionSpec as P

CAP = 4
MESH = pl.DeviceIdType.MESH
LANES = 128
BF16, F32 = jnp.bfloat16, jnp.float32
CROSS = (((1,), (1,)), ((), ()))


def iota(shape, dim):
    return lax.broadcasted_iota(jnp.int32, shape, dim)


def ones_where(mask):
    return jnp.where(mask, 1.0, 0.0).astype(BF16)


def mult(a, b):
    return jnp.dot(a, b, preferred_element_type=F32)


def moe_kernel(
    nodes, n, tok_ref, grad_ref, prob_ref, route_ref, wg_hbm, wu_hbm, wd_hbm, dx_ref, dp_ref,
    wg, wu, wd, outbox, inbox, xs, terms, start, land, ag, pp, acc, outbox2, inbox2,
    w_sem, out_send, out_recv, rs_send, rs_recv, ag_send, ag_recv, back_send, back_recv,
):
    node, me = lax.axis_index("node"), lax.axis_index("local")
    half_ring = n // 2
    slots = nodes * CAP
    rows = slots // 2
    piece = rows // 2
    columns = tok_ref.shape[1]
    rest = columns - LANES
    top, tokens = route_ref.shape
    pairs = top * tokens
    chunk = wg.shape[1] // n
    to = (lax.rem(me + 1, n), lax.rem(me + n - 1, n))

    loads = [
        pltpu.make_async_copy(source, kept, w_sem.at[i])
        for i, (source, kept) in enumerate(((wg_hbm, wg), (wu_hbm, wu), (wd_hbm, wd)))
    ]
    for load in loads:
        load.start()

    barrier = pltpu.get_barrier_semaphore()

    def greet(i, carry):
        pl.semaphore_signal(
            barrier, inc=1, device_id={"node": lax.rem(node + i, nodes)}, device_id_type=MESH
        )
        return carry

    lax.fori_loop(1, nodes, greet, 0)
    for neighbour in to:
        pl.semaphore_signal(barrier, inc=1, device_id={"local": neighbour}, device_id_type=MESH)

    def flat(ref):
        kept = ref[...].astype(F32)
        return jnp.concatenate([kept[k : k + 1] for k in range(top)], axis=1)

    diagonal = iota((pairs, pairs), 0) == iota((pairs, pairs), 1)

    def upright(row):
        return jnp.sum(jnp.where(diagonal, row, 0.0), axis=1, keepdims=True)

    expert_row = flat(route_ref)
    expert_col = upright(expert_row)
    same = expert_row == expert_col
    token_down, token_along = iota((pairs, pairs), 0) % tokens, iota((pairs, pairs), 1) % tokens
    rank_row = jnp.sum(jnp.where(same & (token_down < token_along), 1.0, 0.0), axis=0, keepdims=True)
    rank_col = jnp.sum(jnp.where(same & (token_along < token_down), 1.0, 0.0), axis=1, keepdims=True)
    prob_col = upright(flat(prob_ref))

    blank = jnp.zeros((tokens, LANES - rest), F32)
    lane = iota((pairs, LANES), 1)

    def stacked(block):
        return jnp.concatenate([block] * top, axis=0)

    held_tokens, held_grads = tok_ref[...].astype(F32), grad_ref[...].astype(F32)
    first_blocks = jnp.concatenate([held_tokens[:, 0:LANES], held_grads[:, 0:LANES]], axis=1)
    token_block = jnp.where(
        lane == rest,
        prob_col,
        stacked(jnp.concatenate([held_tokens[:, LANES:columns], blank], axis=1)),
    )
    grad_block = stacked(jnp.concatenate([held_grads[:, LANES:columns], blank], axis=1))
    source = jnp.concatenate(
        [stacked(first_blocks), jnp.concatenate([token_block, grad_block], axis=1)], axis=0
    ).astype(BF16)
    target = (expert_row * (2 * CAP) + rank_row).astype(jnp.int32)
    targets = jnp.concatenate([target, target + CAP], axis=1)
    place = ones_where(iota((2 * slots, 2 * pairs), 0) == targets)
    filled = mult(place, source)
    for part in range(2):
        block = filled[:, part * LANES : (part + 1) * LANES]
        outbox[part] = block.reshape(outbox.shape[1:]).astype(BF16)
        inbox[part, node] = outbox[part, node]

    pl.semaphore_wait(barrier, nodes + 1)

    def beside(i):
        return (1 - 2 * lax.rem(i, 2)) * ((i + 1) // 2)

    def send_body(part, i):
        peer = lax.rem(node + beside(i) + nodes, nodes)
        pltpu.make_async_remote_copy(
            src_ref=outbox.at[part, peer],
            dst_ref=inbox.at[part, node],
            send_sem=out_send.at[part],
            recv_sem=out_recv.at[part],
            device_id={"node": peer},
            device_id_type=MESH,
        ).start()

    for part in range(2):

        def send_part(i, carry, part=part):
            send_body(part, i)
            return carry

        lax.fori_loop(1, nodes, send_part, 0)

    down, along = iota((slots, slots), 0), iota((slots, slots), 1)
    sender, rest_of = along // (2 * CAP), along % (2 * CAP)
    order_in = ones_where(down == rows * (rest_of // CAP) + CAP * sender + rest_of % CAP)
    sender2, rest_of2 = down // (2 * CAP), down % (2 * CAP)
    order_out = ones_where(along == rows * (rest_of2 // CAP) + CAP * sender2 + rest_of2 % CAP)
    target2 = (expert_col * (2 * CAP) + rank_col).astype(jnp.int32)
    targets2 = jnp.concatenate([target2, target2 + CAP], axis=0)
    pick = ones_where(iota((2 * pairs, 2 * slots), 1) == targets2)

    for load in loads:
        load.wait()

    def all_of(send, recv, source, into):
        return pltpu.make_async_remote_copy(
            src_ref=source.at[pl.ds(0, nodes - 1)],
            dst_ref=into.at[pl.ds(0, nodes - 1)],
            send_sem=send,
            recv_sem=recv,
            device_id={"node": lax.rem(node + 1, nodes)},
            device_id_type=MESH,
        )

    def all_out(part):
        return all_of(out_send.at[part], out_recv.at[part], outbox.at[part], inbox.at[part])

    def receive(part):
        all_out(part).wait_recv()
        arrived = inbox[part].astype(F32).reshape(2 * slots, LANES).astype(BF16)
        mixed = mult(
            order_in, jnp.concatenate([arrived[0:slots], arrived[slots : 2 * slots]], axis=1)
        ).astype(BF16)
        for g in range(2):
            for j in range(2):
                column = LANES * (2 * part + j)
                xs[g * rows : (g + 1) * rows, column : column + LANES] = mixed[
                    j * rows : (j + 1) * rows, g * LANES : (g + 1) * LANES
                ]

    def wrap(c):
        return lax.rem(c + 2 * n, n)

    def span(c):
        return pl.ds(pl.multiple_of(c * chunk, chunk), chunk)

    def term(m, c):
        if m == 2:
            return mult(xs[:, 2 * LANES : 2 * LANES + columns], wd[:, span(c)])
        return mult(xs[:, 0:columns], (wg, wu)[m][:, span(c)])

    def own_rows(h):
        return pl.ds(h * rows, rows)

    def rs_copy(d, s, h, m, source):
        return pltpu.make_async_remote_copy(
            src_ref=source,
            dst_ref=land.at[d, s, h, m],
            send_sem=rs_send.at[d, s, h, m],
            recv_sem=rs_recv.at[d, s, h, m],
            device_id={"local": to[d]},
            device_id_type=MESH,
        )

    def chunks_at(s):
        return (wrap(me + half_ring - s), wrap(me - half_ring + s))

    def terms_for(s, kinds):
        for d, c in enumerate(chunks_at(s)):
            for m in kinds:
                terms[d, m] = term(m, c)

    longer = ((0, 0), (1, 1))
    shorter = ((0, 1), (1, 0))

    def begin(d, s, h, m, own):
        start[d, h, m] = own.astype(BF16)
        rs_copy(d, s, h, m, start.at[d, h, m]).start()

    def go_on(d, s, h, m):
        held = land.at[d, s - 1, h, m]
        rs_copy(d, s - 1, h, m, held).wait_recv()
        held[...] = (terms[d, m, own_rows(h)] + held[...].astype(F32)).astype(BF16)
        rs_copy(d, s, h, m, held).start()

    for kinds in ((0, 1), (2,)):
        receive(0 if 0 in kinds else 1)
        for m in kinds:
            both = term(m, wrap(me + half_ring))
            for d, h in longer:
                begin(d, 0, h, m, both[h * rows : (h + 1) * rows])
        terms_for(1, kinds)
        for m in kinds:
            for d, h in shorter:
                begin(d, 1, h, m, terms[d, m, own_rows(h)])
    for m in range(3):
        for d, h in longer:
            go_on(d, 1, h, m)

    def rs_body(s, carry):
        terms_for(s, range(3))
        for h in range(2):
            for m in range(3):
                for d in range(2):
                    go_on(d, s, h, m)
        return carry

    lax.fori_loop(2, half_ring, rs_body, 0)
    for m in range(3):
        terms[0, m] = term(m, me)

    order = (0, 1, 2, 4, 3)

    def is_longer(d, q):
        return d == (0 if q < 2 else 1)

    def ag_copy(d, t, q, c):
        block = pp.at[c] if q == 4 else ag.at[c, pl.ds(q * piece, piece)]
        return pltpu.make_async_remote_copy(
            src_ref=block,
            dst_ref=block,
            send_sem=ag_send.at[d, t, q],
            recv_sem=ag_recv.at[d, t, q],
            device_id={"local": to[d]},
            device_id_type=MESH,
        )

    def sent_at(d, t):
        return wrap(me - t) if d == 0 else wrap(me + t)

    def ag_wait(d, t, q):
        ag_copy(d, t, q, sent_at(d, t + 1)).wait_recv()

    def product(c, first, count):
        weights = jnp.concatenate([wg[:, span(c)], wu[:, span(c)]], axis=1)
        return lax.dot_general(
            ag[c, pl.ds(first, count)], weights, CROSS, preferred_element_type=F32
        )

    last = half_ring - 1
    ones = jnp.ones((8, chunk), BF16)
    whole = []
    for q in range(4):
        h, own = q // 2, slice((q % 2) * piece, (q % 2 + 1) * piece)
        sums = []
        for m in range(3):
            total = terms[0, m, pl.ds(q * piece, piece)]
            for d in range(2):
                if q % 2 == 0:
                    rs_copy(d, last, h, m, land.at[d, last, h, m]).wait_recv()
                total = total + land[d, last, h, m, own].astype(F32)
            sums.append(total)
        gate, up, back = sums
        prob = xs[pl.ds(q * piece, piece), columns : columns + 1].astype(F32)
        squash = jax.nn.sigmoid(gate)
        gated = gate * squash
        hidden = back * prob
        grad_gate = hidden * up * squash * (1.0 + gate * (1.0 - squash))
        ag[me, pl.ds(q * piece, piece)] = jnp.concatenate(
            [grad_gate, hidden * gated], axis=1
        ).astype(BF16)
        whole.append(gated * up * back)
        if q < 3:
            for d in range(2):
                ag_copy(d, 0, q, me).start()
        if q % 2 == 1:
            both = jnp.concatenate(whole[q - 1 :], axis=0)
            high = both.astype(BF16)
            low = (both - high.astype(F32)).astype(BF16)
            part = lax.dot_general(ones, high, CROSS, preferred_element_type=F32) + lax.dot_general(
                ones, low, CROSS, preferred_element_type=F32
            )
            pp[me, 4 * h : 4 * h + 4] = part[0:4]
    for q in (4, 3):
        for d in range(2):
            ag_copy(d, 0, q, me).start()
    acc[...] = product(me, 0, slots)

    def ag_step(t, all_forwarded):
        for q in order:
            for d in range(2):
                ag_wait(d, t - 1, q)
                if all_forwarded or is_longer(d, q):
                    ag_copy(d, t, q, sent_at(d, t)).start()
        acc[...] += product(sent_at(0, t), 0, slots) + product(sent_at(1, t), 0, slots)

    def ag_body(t, carry):
        ag_step(t, True)
        return carry

    lax.fori_loop(1, half_ring - 1, ag_body, 0)
    ag_step(half_ring - 1, False)

    def back_copy(peer):
        return pltpu.make_async_remote_copy(
            src_ref=outbox2.at[peer],
            dst_ref=inbox2.at[node],
            send_sem=back_send,
            recv_sem=back_recv,
            device_id={"node": peer},
            device_id_type=MESH,
        )

    farthest = wrap(me + half_ring)
    for h in range(2):
        for q in (2 * h, 2 * h + 1):
            ag_wait(h, last, q)
        total = acc[own_rows(h)] + product(farthest, h * rows, rows)
        if h == 0:
            ag_wait(1, last, 4)
            weight_sums = jnp.sum(pp[...], axis=0)
        spread = jnp.transpose(jnp.broadcast_to(weight_sums[4 * h : 4 * h + 1], (LANES, rows)))
        stack = jnp.concatenate(
            [
                total[:, 0:LANES],
                jnp.concatenate([total[:, LANES:columns], spread[:, rest:LANES]], axis=1),
            ],
            axis=0,
        ).astype(BF16)
        half = nodes // 2
        outbox2[h * half : (h + 1) * half] = (
            mult(order_out, stack).reshape((half,) + outbox2.shape[1:]).astype(BF16)
        )

        def back_body(i, carry, h=h, half=half):
            peer = h * half + lax.rem(node + beside(i) + nodes, half)

            @pl.when(peer != node)
            def _():
                back_copy(peer).start()

            return carry

        lax.fori_loop(0, half, back_body, 0)
    inbox2[node] = outbox2[node]

    def drain(s, rs_streams, ag_all):
        for d, h in rs_streams:
            for m in range(3):
                rs_copy(d, s, h, m, land.at[d, s, h, m]).wait_send()
        for q in order:
            for d in range(2):
                if ag_all or is_longer(d, q):
                    ag_copy(d, s, q, me).wait_send()

    drain(0, longer, True)

    def drain_body(s, carry):
        drain(s, longer + shorter, True)
        return carry

    lax.fori_loop(1, half_ring - 1, drain_body, 0)
    drain(half_ring - 1, longer + shorter, False)
    for part in range(2):
        all_out(part).wait_send()

    all_of(back_send, back_recv, outbox2, inbox2).wait_recv()
    returned = inbox2[...].astype(F32).reshape(2 * slots, LANES).astype(BF16)
    picked = mult(pick, returned)
    low_sum, high_sum = picked[0:tokens], picked[pairs : pairs + tokens]
    for k in range(1, top):
        low_sum += picked[k * tokens : (k + 1) * tokens]
        high_sum += picked[pairs + k * tokens : pairs + (k + 1) * tokens]
    dx_ref[:, 0:LANES] = low_sum
    dx_ref[:, LANES:columns] = high_sum[:, 0:rest]
    prob_grad = picked[pairs : 2 * pairs, rest : rest + 1]
    along_row = jnp.sum(jnp.where(diagonal, prob_grad, 0.0), axis=0, keepdims=True)
    dp_ref[...] = jnp.concatenate(
        [along_row[:, k * tokens : (k + 1) * tokens] for k in range(top)], axis=0
    )

    all_of(back_send, back_recv, outbox2, inbox2).wait_send()


def on_device(tokens, grad_out, route_prob, route_expert, w_gate, w_up, w_down):
    nodes, n = lax.axis_size("node"), lax.axis_size("local")
    slots = nodes * CAP
    width, hidden = w_gate.shape[1:]
    rows, chunk, half_ring = slots // 2, hidden // n, n // 2
    vmem, hbm = pl.BlockSpec(memory_space=pltpu.VMEM), pl.BlockSpec(memory_space=pl.ANY)
    block_tokens, top = route_expert.shape
    dma = pltpu.SemaphoreType.DMA
    grad_tokens, grad_prob = pl.pallas_call(
        functools.partial(moe_kernel, nodes, n),
        out_shape=(
            jax.ShapeDtypeStruct(tokens.shape, F32),
            jax.ShapeDtypeStruct((top, block_tokens), F32),
        ),
        in_specs=[vmem] * 4 + [hbm] * 3,
        out_specs=(vmem, vmem),
        scratch_shapes=[
            pltpu.VMEM((width, hidden), BF16),
            pltpu.VMEM((width, hidden), BF16),
            pltpu.VMEM((width, hidden), BF16),
            pltpu.VMEM((2, nodes, 2 * CAP, LANES), BF16),
            pltpu.VMEM((2, nodes, 2 * CAP, LANES), BF16),
            pltpu.VMEM((slots, 4 * LANES), BF16),
            pltpu.VMEM((2, 3, slots, chunk), F32),
            pltpu.VMEM((2, 2, 3, rows, chunk), BF16),
            pltpu.VMEM((2, half_ring, 2, 3, rows, chunk), BF16),
            pltpu.VMEM((n, slots, 2 * chunk), BF16),
            pltpu.VMEM((n, 8, LANES), F32),
            pltpu.VMEM((slots, width), F32),
            pltpu.VMEM((nodes, 2 * CAP, LANES), BF16),
            pltpu.VMEM((nodes, 2 * CAP, LANES), BF16),
            dma((3,)),
            dma((2,)),
            dma((2,)),
            dma((2, half_ring, 2, 3)),
            dma((2, half_ring, 2, 3)),
            dma((2, half_ring, 5)),
            dma((2, half_ring, 5)),
            dma,
            dma,
        ],
        compiler_params=pltpu.CompilerParams(
            collective_id=0, has_side_effects=True, vmem_limit_bytes=56 * 1024 * 1024
        ),
    )(
        tokens,
        grad_out,
        route_prob.T,
        route_expert.T,
        w_gate[0],
        w_up[0],
        jnp.swapaxes(w_down[0], 0, 1),
    )
    return grad_tokens.astype(BF16), grad_prob.T.astype(BF16)


def solution(mesh):
    return jax.shard_map(
        on_device,
        mesh=mesh,
        in_specs=(
            P("node", "local"),
            P("node", "local"),
            P("node", None),
            P("node", None),
            P("node", "local", None),
            P("node", "local", None),
            P("node", None, "local"),
        ),
        out_specs=(P("node", "local"), P("node", None)),
        check_vma=False,
    )
```
